256 devices in a mesh: feat: 32 (over z_lo, x, core), ex: 8 (over z_hi, y).
Axes of the slice: x: 4, y: 4, z: 8 (z_hi: 2, z_lo: 4; z = z_hi * 4 + z_lo), core: 2. Of those that a mesh axis runs over, the one named last changes fastest.
Arguments:
- activations: bfloat16 [8, 128, 4096], P('ex', None, 'feat'), may hold values from -6 to 6
- output_grads: bfloat16 [8, 128, 14336], P('ex', None, 'feat'), may hold values from -0.52734375 to 0.52734375
- counts: int32 [8], P('ex'), may hold values from 1 to 128
- sign_words: int32 [128, 547], replicated, may hold values from 0 to 1073741823
- coord_row: int32 [4096], replicated, may hold values from 0 to 4095
- coord_col: int32 [4096], replicated, may hold values from 0 to 16383
- queries: float32 [1024, 4096], P('feat', 'ex'), may hold values from -6 to 6
Outputs:
- projected: float32 [8, 4096], P('ex')
- scores: float32 [8, 1024], P('ex', 'feat')
The draws below stay inside these ranges and needn't reach their ends.
Inputs may be any that keep to these rules, and one draw needn't show every extreme that they name: `sign_words`: bits 0 to 29 of each word are signs; columns past 16384 are unused.
All inputs are finite; a program needn't handle non-finite values.
Results may differ from the reference program's by a relative error of at most 0.0003.
Values may be sent and summed in bfloat16 or wider, within the bound.
No kernel may reach another device: no remote copies, remote signals or barrier semaphores. Data moves between devices by JAX's collectives and lax.ppermute only.
A program may use at most 128 MiB of HBM per device.

```python
import math
import jax
import jax.numpy as jnp
from jax import lax

DIN = 4096
DOUT = 14336
DPAD = 16384
SIGN_ROWS = 128
TOK = 128
PROJ = 4096
NQUERY = 1024
EXAMPLES = 8
WORDS = 547


def set_ends(result, stream_key, least, largest):
    spot = [jax.random.randint(jax.random.fold_in(stream_key, axis), (), 0, length) for axis, length in enumerate(result.shape)]
    longest = result.shape.index(max(result.shape))
    neighbour = spot[:longest] + [(spot[longest] + 1) % result.shape[longest]] + spot[longest + 1:]
    return result.at[tuple(spot)].set(least).at[tuple(neighbour)].set(largest)


def levels(stream_key, shape, split, smallest, high):
    level, own = 1.0, jax.random.fold_in(stream_key, 6)
    for dim, shards_of in split:
        steps = jnp.exp(jax.random.uniform(jax.random.fold_in(own, dim), (shards_of,), jnp.float32, smallest / len(split), high / len(split)))
        level = level * jnp.repeat(steps, shape[dim] // shards_of).reshape([-1 if axis == dim else 1 for axis in range(len(shape))])
    return level


def bell_draw(key, extent, deviation, most, shards=(), kind=jnp.bfloat16):
    factor_of = levels(key, extent, shards, -0.22, 0.18) if shards else 1.0
    drawn = jax.random.normal(key, extent, jnp.float32) * deviation * factor_of
    return jnp.minimum(jnp.maximum(drawn, -most), most).astype(kind)


def setup_inputs(seed: int = 0) -> dict:
    splits = jax.random.split(jax.random.key(seed), 8)
    activations = bell_draw(splits[0], (EXAMPLES, TOK, DIN), 1.0, 6.0, ((0, 8), (2, 32)))
    output_grads = bell_draw(splits[1], (EXAMPLES, TOK, DOUT), 0.088, 0.52734375, ((0, 8), (2, 32)))
    counts = set_ends(jax.random.randint(splits[2], (EXAMPLES,), 1, TOK + 1), jax.random.fold_in(splits[2], 1), 1, TOK).astype(jnp.int32)
    sign_words = set_ends(jax.random.randint(splits[3], (SIGN_ROWS, WORDS), 0, 1073741824), jax.random.fold_in(splits[3], 1), 0, 1073741823).astype(jnp.int32)
    coord_row = set_ends(jax.random.randint(splits[4], (PROJ,), 0, DIN), jax.random.fold_in(splits[4], 1), 0, DIN - 1).astype(jnp.int32)
    coord_col = set_ends(jax.random.randint(splits[5], (PROJ,), 0, DPAD), jax.random.fold_in(splits[5], 1), 0, DPAD - 1).astype(jnp.int32)
    queries = bell_draw(splits[6], (NQUERY, PROJ), 1.0, 6.0, ((0, 32), (1, 8)), jnp.float32)
    return {"activations": activations, "output_grads": output_grads, "counts": counts, "sign_words": sign_words, "coord_row": coord_row, "coord_col": coord_col, "queries": queries}


def parity_signs(left_ids, right_ids, bit_count):
    common = jnp.bitwise_and(left_ids, right_ids)
    running = jnp.zeros(common.shape, jnp.int32)
    for position in range(bit_count):
        running = running + jnp.bitwise_and(jnp.right_shift(common, position), 1)
    return (1 - 2 * jnp.bitwise_and(running, 1)).astype(jnp.float32)

def sylvester(order_size):
    indices = jnp.arange(order_size, dtype=jnp.int32)
    return parity_signs(indices[:, None], indices[None, :], order_size.bit_length() - 1)

def walsh_axis(field, dim_at):
    length = field.shape[dim_at]
    factors = []
    remain = length
    while remain > 1:
        factor = min(remain, 128)
        factors.append(factor)
        remain = remain // factor
    leading = field.shape[:dim_at]
    trailing = field.shape[dim_at + 1:]
    reshaped = field.reshape(leading + tuple(factors) + trailing)
    labels = 'abcdefghijklmnopqrstuvw'[:reshaped.ndim]
    for place, factor in enumerate(factors):
        target = dim_at + place
        result_labels = labels[:target] + 'z' + labels[target + 1:]
        reshaped = jnp.einsum(labels + ',' + labels[target] + 'z->' + result_labels, reshaped, sylvester(factor), precision=lax.Precision.HIGHEST)
    return reshaped.reshape(field.shape)

def unpack_signs(sign_words, length):
    shifts = jnp.arange(30, dtype=jnp.int32)
    bit_values = jnp.bitwise_and(jnp.right_shift(sign_words[:, :, None], shifts), 1)
    unpacked = bit_values.reshape(sign_words.shape[0], sign_words.shape[1] * 30)[:, :length]
    return (1 - 2 * unpacked).astype(jnp.float32)

def reference(activations, output_grads, counts, sign_words, coord_row, coord_col, queries):
    sign_table = unpack_signs(sign_words, DPAD)
    tiled = jnp.tile(sign_table, (DIN // SIGN_ROWS, 1))
    row_signs = parity_signs(jnp.arange(DIN, dtype=jnp.int32)[:, None], coord_row[None, :], DIN.bit_length() - 1)
    norm_scale = 1.0 / math.sqrt(DIN * DPAD)

    def project_one(items):
        token_acts, token_grads, token_count = items
        live_mask = (jnp.arange(TOK, dtype=jnp.int32) < token_count).astype(jnp.bfloat16)
        token_acts = token_acts * live_mask[:, None]
        gradient = jnp.dot(token_acts.T, token_grads, preferred_element_type=jnp.float32)
        signed = jnp.pad(gradient, ((0, 0), (0, DPAD - DOUT))) * tiled
        mixed_field = walsh_axis(signed, 1)
        picked = mixed_field[:, coord_col]
        return lax.optimization_barrier(jnp.sum(row_signs * picked, axis=0)) * norm_scale
    projected = lax.map(project_one, (activations, output_grads, counts))
    scores = jnp.dot(projected, queries.T, precision=lax.Precision.HIGHEST) * (1.0 / math.sqrt(PROJ))
    return (projected, scores)
```

```python
import math

import jax
import jax.numpy as jnp
from jax import lax
from jax.experimental import pallas as pl
from jax.experimental.pallas import tpu as pltpu
from jax.sharding import PartitionSpec as P

DIN = 4096
DPAD = 16384
PROJ = 4096
TOK = 128
COLS = 448
RUNS = COLS // 64
GROUPS = 8
BLK = 256
MAXB = 24
HOTS = 32

ROW_STEPS = (16, 8, 6)
COL_STEPS = (1, 2)
SUM_STEPS = (1, 2, 6, 8, 16)
EX_STEPS = (4, 1, 3)

F32 = jnp.float32
BF16 = jnp.bfloat16
I32 = jnp.int32
NT = (((1,), (1,)), ((), ()))


def iota(shape, dim):
    return lax.broadcasted_iota(I32, shape, dim)


def parity(bits):
    bits = bits ^ (bits >> 4)
    bits = bits ^ (bits >> 2)
    bits = bits ^ (bits >> 1)
    return bits & 1


def sign_of(bit):
    return (1 - 2 * bit).astype(F32)


def one_hot(cond):
    return jnp.where(cond, 1.0, 0.0)


def sort_kernel(row_ref, col_ref, sorted_ref, low_ref, high_ref, info_ref, value_ref):
    row = row_ref[...]
    col = col_ref[...]
    block_row = row >> 7
    key = (
        ((block_row >> 4) & 1)
        | (((block_row >> 3) & 1) << 1)
        | ((((block_row >> 1) ^ (block_row >> 2)) & 1) << 2)
    )
    hot = jnp.concatenate([one_hot(key == g) for g in range(GROUPS)], axis=0).astype(BF16)
    upper = one_hot(iota((128, 128), 0) <= iota((128, 128), 1)).astype(BF16)
    within = jnp.dot(hot, upper, preferred_element_type=F32)
    sums = jnp.dot(hot, jnp.ones((128, 128), BF16), preferred_element_type=F32)
    here, there = iota((256, 256), 0), iota((256, 256), 1)
    earlier = one_hot(((here >> 5) == (there >> 5)) & (there < here)).astype(BF16)
    before = jnp.dot(earlier, sums.astype(BF16), preferred_element_type=F32)
    rank = within + before - 1.0
    lane = iota((1, 128), 1)
    base = jnp.zeros((1, 128), I32)
    owner = jnp.zeros((1, 128), I32)
    place = jnp.zeros((32, 128), F32)
    for g in range(GROUPS):
        last = 32 * g + 31
        total = (before[last : last + 1] + sums[last : last + 1]).astype(I32)
        place = place + jnp.where(
            key == g, rank[32 * g : 32 * g + 32] + (base << 8).astype(F32), 0.0
        )
        base = base + ((total + (BLK - 1)) >> 8)
        owner = owner + jnp.where(base <= lane, 1, 0)
    info_ref[...] = jnp.concatenate([owner, base, jnp.zeros((6, 128), I32)], axis=0)
    place = place.astype(I32)
    for i in range(32):
        at = slice(128 * i, 128 * i + 128)
        spot = place[i : i + 1]
        low_ref[:, at] = one_hot(iota((BLK, 128), 0) == (spot & (BLK - 1))).astype(BF16)
        high = one_hot(iota((HOTS, 128), 0) == (spot >> 8))
        high_ref[:, at] = high.astype(BF16)
        r, c = row[i : i + 1], col[i : i + 1]
        fields = (r & 127, r >> 7, c >> 6, c & 63)
        value_ref[:, at] = jnp.concatenate(
            [high * field.astype(F32) for field in fields], axis=0
        ).astype(BF16)
    sorted_ref[...] = lax.dot_general(
        value_ref[...], low_ref[...], NT, preferred_element_type=F32
    ).astype(I32)


def sort_coords(coord_row, coord_col):
    return pl.pallas_call(
        sort_kernel,
        out_shape=(
            jax.ShapeDtypeStruct((4 * HOTS, BLK), I32),
            jax.ShapeDtypeStruct((BLK, PROJ), BF16),
            jax.ShapeDtypeStruct((HOTS, PROJ), BF16),
            jax.ShapeDtypeStruct((8, 128), I32),
        ),
        scratch_shapes=[pltpu.VMEM((4 * HOTS, PROJ), BF16)],
        cost_estimate=pl.CostEstimate(flops=10**9, bytes_accessed=3 * 10**6, transcendentals=0),
        name="sort_coords",
    )(coord_row.reshape(32, 128), coord_col.reshape(32, 128))


def coord_signs_kernel(place_ref, sorted_ref, u_ref, vl_ref, vj_ref):
    feat = place_ref[0]

    def step(b, carry):
        low_row = sorted_ref[pl.ds(b, 1), :]
        block_row = sorted_ref[pl.ds(HOTS + b, 1), :]
        col_high = sorted_ref[pl.ds(2 * HOTS + b, 1), :]
        col_low = sorted_ref[pl.ds(3 * HOTS + b, 1), :]
        u_ref[b] = sign_of(parity(iota((128, BLK), 0) & low_row)).astype(BF16)
        flip = parity(block_row & feat)
        vl_ref[b] = sign_of(parity(iota((64, BLK), 0) & col_low) ^ flip) * (
            1.0 / math.sqrt(DIN * DPAD)
        )
        piece = iota((32, BLK), 0)
        run = RUNS * (feat ^ (piece >> 3)) + (piece & 7)
        vj_ref[b] = sign_of(parity(run & col_high))
        return carry

    lax.fori_loop(0, MAXB, step, 0)


def coord_signs(place, sorted_fields):
    return pl.pallas_call(
        coord_signs_kernel,
        out_shape=(
            jax.ShapeDtypeStruct((MAXB, 128, BLK), BF16),
            jax.ShapeDtypeStruct((MAXB, 64, BLK), F32),
            jax.ShapeDtypeStruct((MAXB, 32, BLK), F32),
        ),
        in_specs=[
            pl.BlockSpec(memory_space=pltpu.SMEM),
            pl.BlockSpec(memory_space=pltpu.VMEM),
        ],
        cost_estimate=pl.CostEstimate(flops=10**9, bytes_accessed=4 * 10**6, transcendentals=0),
        name="coord_signs",
    )(place, sorted_fields)


def table_kernel(place_ref, words_ref, sign_ref):
    feat = place_ref[0]
    words = words_ref[...]
    octets = jnp.concatenate(
        [((words >> (8 * p)) & 255).astype(F32) for p in range(4)], axis=1
    ).astype(BF16)
    first_word = ((4 * COLS * (feat >> 2)) * 34953) >> 20
    for e in range(4):
        col = COLS * (feat ^ e) + iota((COLS, 128), 0)
        word = (col * 34953) >> 20
        bit = col - 30 * word
        target = ((bit >> 3) << 6) + (word - first_word)
        lane = iota((COLS, 128), 1)
        pick = jnp.concatenate(
            [one_hot(lane == target), one_hot(lane + 128 == target)], axis=1
        ).astype(BF16)
        octet = lax.dot_general(pick, octets, NT, preferred_element_type=F32).astype(I32)
        sign_ref[e] = sign_of((octet >> (bit & 7)) & 1)


def sign_table(place, words):
    return pl.pallas_call(
        table_kernel,
        out_shape=jax.ShapeDtypeStruct((4, COLS, 128), F32),
        in_specs=[
            pl.BlockSpec(memory_space=pltpu.SMEM),
            pl.BlockSpec(memory_space=pltpu.VMEM),
        ],
        cost_estimate=pl.CostEstimate(flops=10**9, bytes_accessed=10**6, transcendentals=0),
        name="sign_table",
    )(place, words)


def split(value):
    high = value.astype(BF16)
    return high, (value - high.astype(F32)).astype(BF16)


def main_kernel(
    info_ref, a_ref, g_ref, sign_ref, u_ref, vl_ref, vj_ref, out_ref, mixed_ref, signed_ref
):
    for first in range(0, TOK, 32):
        rows = slice(first, first + 32)
        parts = [a_ref[i, rows, :].astype(F32) for i in range(GROUPS)]
        for bit in (1, 2, 4):
            for i in range(GROUPS):
                if not i & bit:
                    parts[i], parts[i | bit] = (
                        parts[i] + parts[i | bit],
                        parts[i] - parts[i | bit],
                    )
        for i in range(GROUPS):
            high, low = split(parts[i])
            mixed_ref[rows, 128 * i : 128 * i + 128] = high
            mixed_ref[TOK + first : TOK + first + 32, 128 * i : 128 * i + 128] = low
    for e in range(4):
        grads = jnp.concatenate([g_ref[e], g_ref[e]], axis=1)
        signs = sign_ref[e]
        here = slice(COLS * e, COLS * e + COLS)
        for pair in range(GROUPS // 2):
            outer = jnp.dot(
                grads, mixed_ref[:, 256 * pair : 256 * pair + 256], preferred_element_type=F32
            )
            for half in range(2):
                high, low = split(outer[:, 128 * half : 128 * half + 128] * signs)
                signed_ref[2 * pair + half, here, 0:128] = high
                signed_ref[2 * pair + half, here, 128:256] = low
    out_ref[...] = jnp.zeros_like(out_ref)

    def block(b, carry):
        group = info_ref[0, b]
        weights = jnp.concatenate([u_ref[b], u_ref[b]], axis=0)
        total = jnp.zeros((64, BLK), F32)
        for e in range(4):
            here = slice(COLS * e, COLS * e + COLS)
            rows = jnp.dot(signed_ref[group, here, :], weights, preferred_element_type=F32)
            for j in range(RUNS):
                total = total + vj_ref[b, 8 * e + j : 8 * e + j + 1, :] * rows[64 * j : 64 * j + 64]
        out_ref[pl.ds(b, 1), :] = jnp.sum(total * vl_ref[b], axis=0, keepdims=True)
        return carry

    lax.fori_loop(0, info_ref[1, 0], block, 0)


def partial_sums(info, acts, grads, signs, u, vl, vj):
    vmem = pl.BlockSpec(memory_space=pltpu.VMEM)
    return pl.pallas_call(
        main_kernel,
        out_shape=jax.ShapeDtypeStruct((MAXB, BLK), F32),
        in_specs=[pl.BlockSpec(memory_space=pltpu.SMEM)] + [vmem] * 6,
        out_specs=vmem,
        scratch_shapes=[
            pltpu.VMEM((2 * TOK, GROUPS * 128), BF16),
            pltpu.VMEM((GROUPS, 4 * COLS, 256), BF16),
        ],
        cost_estimate=pl.CostEstimate(flops=10**10, bytes_accessed=10**7, transcendentals=0),
        compiler_params=pltpu.CompilerParams(vmem_limit_bytes=40 * 2**20),
        name="partial_sums",
    )(info, acts, grads, signs, u, vl, vj)


def finish_kernel(place_ref, mine_ref, other_ref, low_ref, high_ref, q_ref, proj_ref, score_ref, row_ref):
    ex = place_ref[1]
    total = mine_ref[...] + other_ref[...]
    total = jnp.concatenate([total, jnp.zeros((HOTS - MAXB, BLK), F32)], axis=0)
    high, low = split(total)
    picked = jnp.dot(
        jnp.concatenate([high, low], axis=0), low_ref[...], preferred_element_type=F32
    )
    picked = (picked[:HOTS] + picked[HOTS:]) * high_ref[...].astype(F32)
    proj = jnp.sum(picked, axis=0, keepdims=True)
    proj_ref[...] = proj
    for s in range(8):
        row_ref[s : s + 1, :] = proj[:, 512 * s : 512 * s + 512]
    order = [0]
    for step in EX_STEPS:
        order = order + [d ^ step for d in order]
    acc = jnp.zeros((32, 512), F32)
    for spot, d in enumerate(order):
        acc = acc + q_ref[spot] * row_ref[pl.ds(ex ^ d, 1), :]
    acc = (acc[:, 0:128] + acc[:, 128:256]) + (acc[:, 256:384] + acc[:, 384:512])
    scores = lax.dot_general(
        jnp.ones((8, 128), F32), acc, NT, precision=lax.Precision.HIGHEST, preferred_element_type=F32
    )
    score_ref[...] = scores[0:1] * (1.0 / math.sqrt(PROJ))


def finish(place, mine, other, low, high, queries):
    vmem = pl.BlockSpec(memory_space=pltpu.VMEM)
    return pl.pallas_call(
        finish_kernel,
        out_shape=(
            jax.ShapeDtypeStruct((1, PROJ), F32),
            jax.ShapeDtypeStruct((1, 32), F32),
        ),
        in_specs=[pl.BlockSpec(memory_space=pltpu.SMEM)] + [vmem] * 5,
        out_specs=(vmem, vmem),
        scratch_shapes=[pltpu.VMEM((8, 512), F32)],
        name="finish",
    )(place, mine, other, low, high, queries)


def swap(value, axis, size, step):
    return lax.ppermute(value, axis, [(i, i ^ step) for i in range(size)])


def gather_by(value, axis, size, steps):
    value = value[None]
    for step in steps:
        value = jnp.concatenate([value, swap(value, axis, size, step)], axis=0)
    return value


def body(activations, output_grads, counts, sign_words, coord_row, coord_col, queries):
    feat = lax.axis_index("feat")
    ex = lax.axis_index("ex")
    place = jnp.stack([feat, ex]).astype(I32)
    live = jnp.arange(TOK, dtype=I32)[:, None] < counts[0]
    own_grads = jnp.where(live, output_grads[0], jnp.zeros((), BF16)).T
    acts = gather_by(activations[0], "feat", 32, ROW_STEPS)
    grads = gather_by(own_grads, "feat", 32, COL_STEPS)
    all_queries = gather_by(queries, "ex", 8, EX_STEPS)

    sorted_fields, low, high, info = sort_coords(coord_row, coord_col)
    u, vl, vj = coord_signs(place, sorted_fields)
    window = lax.dynamic_slice(sign_words, (0, (4 * COLS * (feat // 4)) // 30), (128, 64))
    signs = sign_table(place, window)
    total = partial_sums(info, acts, grads, signs, u, vl, vj)
    for step in SUM_STEPS[:-1]:
        total = total + swap(total, "feat", 32, step)
    other = swap(total, "feat", 32, SUM_STEPS[-1])
    return finish(place, total, other, low, high, all_queries)


def solution(mesh):
    return jax.shard_map(
        body,
        mesh=mesh,
        in_specs=(
            P("ex", None, "feat"),
            P("ex", None, "feat"),
            P("ex"),
            P(),
            P(),
            P(),
            P("feat", "ex"),
        ),
        out_specs=(P("ex", None), P("ex", "feat")),
        check_vma=False,
    )
```

```python
import math

import jax
import jax.numpy as jnp
from jax import lax
from jax.experimental import pallas as pl
from jax.experimental.pallas import tpu as pltpu
from jax.sharding import PartitionSpec as P

DIN = 4096
DPAD = 16384
PROJ = 4096
TOK = 128
COLS = 448
RUNS = COLS // 64
ROW_GROUPS = 8
COL_GROUPS = 8
GROUPS = ROW_GROUPS * COL_GROUPS
BLK = 128
MAXB = 96
UNROLL = 16
PIECES = 4
RUNS_HERE = PIECES * RUNS

ROW_STEPS = (16, 8, 6)
COL_STEPS = (1, 2)
SUM_STEPS = (1, 2, 6, 8, 16)
EX_STEPS = (4, 1, 3)

F32 = jnp.float32
BF16 = jnp.bfloat16
I32 = jnp.int32
NT = (((1,), (1,)), ((), ()))


def iota(shape, dim):
    return lax.broadcasted_iota(I32, shape, dim)


def parity(bits):
    bits = bits ^ (bits >> 4)
    bits = bits ^ (bits >> 2)
    bits = bits ^ (bits >> 1)
    return bits & 1


def parity3(bits):
    return (bits ^ (bits >> 1) ^ (bits >> 2)) & 1


def sign_of(bit):
    return (1 - 2 * bit).astype(F32)


def one_hot(cond):
    return jnp.where(cond, 1.0, 0.0)


def cost(microseconds):
    return pl.CostEstimate(
        flops=int(microseconds * 10**9), bytes_accessed=10**6, transcendentals=0
    )


def rank_kernel(ints_ref, after_ref, place_ref, info_ref, hot_ref, count_ref):
    coord = ints_ref[0:32, :]
    block_row = coord >> 21
    key = (
        ((coord >> 3) & 7)
        | (((block_row >> 4) & 1) << 3)
        | (((block_row >> 3) & 1) << 4)
        | ((((block_row >> 1) ^ (block_row >> 2)) & 1) << 5)
    )
    for i in range(32):
        hot_ref[GROUPS * i : GROUPS * i + GROUPS, :] = one_hot(
            iota((GROUPS, 128), 0) == key[i : i + 1]
        ).astype(BF16)
    lane = iota((128, 256), 1)
    upto = one_hot((iota((128, 256), 0) <= lane) | (lane >= 128)).astype(BF16)
    count_ref[...] = jnp.dot(hot_ref[...], upto, preferred_element_type=F32)
    total = jnp.zeros((GROUPS, 128), F32)
    for i in range(32):
        here = slice(GROUPS * i, GROUPS * i + GROUPS)
        count_ref[here, 0:128] = count_ref[here, 0:128] + total
        total = total + count_ref[here, 128:256]
    blocks = ((total.astype(I32) + (BLK - 1)) >> 7).astype(F32)
    earlier = one_hot(iota((GROUPS, GROUPS), 1) < iota((GROUPS, GROUPS), 0)).astype(BF16)
    base = jnp.dot(earlier, blocks.astype(BF16), preferred_element_type=F32)
    upto_here = base + blocks
    ended = one_hot(upto_here <= iota((GROUPS, 128), 1).astype(F32))
    owner = jnp.minimum(jnp.sum(ended, axis=0, keepdims=True), GROUPS - 1.0).astype(I32)
    used = upto_here[GROUPS - 1 : GROUPS].astype(I32)
    info_ref[...] = jnp.concatenate([owner, used, jnp.zeros((6, 128), I32)], axis=0)
    base = base * float(BLK) - 1.0
    for i in range(32):
        here = slice(GROUPS * i, GROUPS * i + GROUPS)
        spot = hot_ref[here, :].astype(F32) * (count_ref[here, 0:128] + base)
        place_ref[i : i + 1, :] = jnp.sum(spot, axis=0, keepdims=True).astype(I32)

def rank_coords(ints, after):
    return pl.pallas_call(
        rank_kernel,
        out_shape=(
            jax.ShapeDtypeStruct((32, 128), I32),
            jax.ShapeDtypeStruct((8, 128), I32),
        ),
        in_specs=[pl.BlockSpec(memory_space=pltpu.VMEM), pl.BlockSpec(memory_space=pl.ANY)],
        scratch_shapes=[
            pltpu.VMEM((GROUPS * 32, 128), BF16),
            pltpu.VMEM((GROUPS * 32, 256), F32),
        ],
        compiler_params=pltpu.CompilerParams(vmem_limit_bytes=8 * 2**20),
        cost_estimate=cost(1),
        name="rank_coords",
    )(ints, after)


def sort_kernel(
    coord_ref, place_ref, after_ref, after_too_ref, sorted_ref, low_ref, high_ref, value_ref
):
    for i in range(32):
        at = slice(128 * i, 128 * i + 128)
        spot, coord = place_ref[i : i + 1, :], coord_ref[i : i + 1, :]
        low_ref[:, at] = one_hot(iota((BLK, 128), 0) == (spot & (BLK - 1))).astype(BF16)
        high = one_hot(iota((MAXB, 128), 0) == (spot >> 7))
        high_ref[:, at] = high.astype(BF16)
        fields = ((coord >> 14) & 127, (coord >> 6) & 255, ((coord >> 21) << 3) | (coord & 7))
        for n, field in enumerate(fields):
            value_ref[MAXB * n : MAXB * n + MAXB, at] = (high * field.astype(F32)).astype(BF16)
    sorted_ref[...] = lax.dot_general(
        value_ref[...], low_ref[...], NT, preferred_element_type=F32
    ).astype(I32)


def sort_coords(coord, place, after, after_too):
    vmem = pl.BlockSpec(memory_space=pltpu.VMEM)
    return pl.pallas_call(
        sort_kernel,
        out_shape=(
            jax.ShapeDtypeStruct((3 * MAXB, BLK), I32),
            jax.ShapeDtypeStruct((BLK, PROJ), BF16),
            jax.ShapeDtypeStruct((MAXB, PROJ), BF16),
        ),
        in_specs=[vmem] * 2 + [pl.BlockSpec(memory_space=pl.ANY)] * 2,
        scratch_shapes=[pltpu.VMEM((3 * MAXB, PROJ), BF16)],
        compiler_params=pltpu.CompilerParams(vmem_limit_bytes=8 * 2**20),
        cost_estimate=cost(2),
        name="sort_coords",
    )(coord, place, after, after_too)


def coord_signs_kernel(info_ref, sorted_ref, after_ref, u_ref, vl_ref, vj_ref):
    feat = lax.axis_index("feat")
    run = iota((32, BLK), 0)
    piece = (run * 37) >> 8
    run = RUNS * (feat ^ piece) + (run - RUNS * piece)
    eight = iota((8, BLK), 0)

    def step(i, carry):
        for n in range(UNROLL):
            b = i * UNROLL + n
            row = sorted_ref[pl.ds(b, 1), :]
            col_high = sorted_ref[pl.ds(MAXB + b, 1), :]
            rest = sorted_ref[pl.ds(2 * MAXB + b, 1), :]
            column = [sign_of(parity3(eight & row))]
            for bit in range(3, 7):
                turn = sign_of((row >> bit) & 1)
                column = column + [part * turn for part in column]
            u_ref[b] = jnp.concatenate(column, axis=0).astype(BF16)
            flip = parity((rest >> 3) & feat)
            vl_ref[b] = sign_of(parity3(eight & rest) ^ flip) * (1.0 / math.sqrt(DIN * DPAD))
            vj_ref[b] = sign_of(parity(run & col_high))
        return carry

    lax.fori_loop(0, (info_ref[1, 0] + (UNROLL - 1)) // UNROLL, step, 0)


def coord_signs(info, sorted_fields, after):
    return pl.pallas_call(
        coord_signs_kernel,
        out_shape=(
            jax.ShapeDtypeStruct((MAXB, 128, BLK), BF16),
            jax.ShapeDtypeStruct((MAXB, 8, BLK), F32),
            jax.ShapeDtypeStruct((MAXB, 32, BLK), F32),
        ),
        in_specs=[
            pl.BlockSpec(memory_space=pltpu.SMEM),
            pl.BlockSpec(memory_space=pltpu.VMEM),
            pl.BlockSpec(memory_space=pl.ANY),
        ],
        compiler_params=pltpu.CompilerParams(vmem_limit_bytes=8 * 2**20),
        cost_estimate=cost(3),
        name="coord_signs",
    )(info, sorted_fields, after)


def table_kernel(words_ref, after_ref, sign_ref):
    feat = lax.axis_index("feat")
    first_word = ((PIECES * COLS * (feat >> 2)) * 34953) >> 20
    words = words_ref[pl.ds(first_word, 64), :]
    octets = jnp.concatenate(
        [((words >> (8 * p)) & 255).astype(F32) for p in range(4)], axis=0
    ).astype(BF16)
    for e in range(PIECES):
        col = COLS * (feat ^ e) + iota((COLS, 128), 0)
        word = (col * 34953) >> 20
        bit = col - 30 * word
        target = ((bit >> 3) << 6) + (word - first_word)
        lane = iota((COLS, 128), 1)
        pick = jnp.concatenate(
            [one_hot(lane == target), one_hot(lane + 128 == target)], axis=1
        ).astype(BF16)
        octet = jnp.dot(pick, octets, preferred_element_type=F32).astype(I32)
        sign_ref[COLS * e : COLS * e + COLS, :] = sign_of((octet >> (bit & 7)) & 1)


def sign_table(words, after):
    return pl.pallas_call(
        table_kernel,
        out_shape=jax.ShapeDtypeStruct((PIECES * COLS, 128), F32),
        in_specs=[pl.BlockSpec(memory_space=pltpu.VMEM), pl.BlockSpec(memory_space=pl.ANY)],
        compiler_params=pltpu.CompilerParams(vmem_limit_bytes=8 * 2**20),
        cost_estimate=cost(2),
        name="sign_table",
    )(words, after)


def butterflies(parts):
    parts = list(parts)
    for bit in (1, 2, 4):
        for i in range(len(parts)):
            if not i & bit:
                one, two = parts[i], parts[i | bit]
                parts[i], parts[i | bit] = one + two, one - two
    return parts


def split(value):
    high = value.astype(BF16)
    return high, (value - high.astype(F32)).astype(BF16)


def main_kernel(
    info_ref, counts_ref, a_ref, g_ref, sign_ref, u_ref, vl_ref, vj_ref, low_ref, high_ref,
    out_ref, mixed_ref, signed_ref, block_ref,
):
    for first in range(0, TOK, 32):
        rows = slice(first, first + 32)
        parts = [a_ref[i, rows, :].astype(F32) for i in range(ROW_GROUPS)]
        live = first + iota((32, 128), 0) < counts_ref[0:1, 0:1]
        parts = [jnp.where(live, part, 0.0) for part in butterflies(parts)]
        for i in range(ROW_GROUPS):
            high, low = split(parts[i])
            mixed_ref[rows, 128 * i : 128 * i + 128] = high
            mixed_ref[TOK + first : TOK + first + 32, 128 * i : 128 * i + 128] = low
    tile = 2 * COLS
    for first in range(0, PIECES * COLS, tile):
        grads = g_ref[first : first + tile, :]
        grads = jnp.concatenate([grads, grads], axis=1)
        for pair in range(ROW_GROUPS // 2):
            outer = jnp.dot(
                grads, mixed_ref[:, 256 * pair : 256 * pair + 256], preferred_element_type=F32
            )
            for half in range(2):
                group = COL_GROUPS * (2 * pair + half)
                for at in range(0, tile, 128):
                    signed = (
                        outer[at : at + 128, 128 * half : 128 * half + 128]
                        * sign_ref[first + at : first + at + 128, :]
                    )
                    runs = [
                        butterflies(
                            [signed[64 * r + 8 * h : 64 * r + 8 * h + 8] for h in range(COL_GROUPS)]
                        )
                        for r in range(2)
                    ]
                    to = (first + at) // 8
                    for h in range(COL_GROUPS):
                        high, low = split(jnp.concatenate([runs[0][h], runs[1][h]], axis=0))
                        signed_ref[group + h, to : to + 16, 0:128] = high
                        signed_ref[group + h, to : to + 16, 128:256] = low
    block_ref[...] = jnp.zeros_like(block_ref)

    def step(i, carry):
        for n in range(UNROLL):
            b = i * UNROLL + n
            weights = jnp.concatenate([u_ref[b], u_ref[b]], axis=0)
            rows = jnp.dot(signed_ref[info_ref[0, b]], weights, preferred_element_type=F32)
            total = vj_ref[b, 0:1, :] * rows[0:8]
            for j in range(1, RUNS_HERE):
                total = total + vj_ref[b, j : j + 1, :] * rows[8 * j : 8 * j + 8]
            block_ref[pl.ds(b, 1), :] = jnp.sum(total * vl_ref[b], axis=0, keepdims=True)
        return carry

    lax.fori_loop(0, (info_ref[1, 0] + (UNROLL - 1)) // UNROLL, step, 0)
    pair = jnp.concatenate(split(block_ref[...]), axis=1)
    for first in range(0, PROJ, 512):
        at = slice(first, first + 512)
        low = low_ref[:, at]
        spread = jnp.dot(pair, jnp.concatenate([low, low], axis=0), preferred_element_type=F32)
        out_ref[:, at] = jnp.sum(spread * high_ref[:, at].astype(F32), axis=0, keepdims=True)


def partial_sums(info, counts, acts, grads, signs, u, vl, vj, low, high):
    vmem = pl.BlockSpec(memory_space=pltpu.VMEM)
    return pl.pallas_call(
        main_kernel,
        out_shape=jax.ShapeDtypeStruct((1, PROJ), F32),
        in_specs=[pl.BlockSpec(memory_space=pltpu.SMEM)] + [vmem] * 9,
        out_specs=vmem,
        scratch_shapes=[
            pltpu.VMEM((2 * TOK, ROW_GROUPS * 128), BF16),
            pltpu.VMEM((GROUPS, RUNS_HERE * 8, 256), BF16),
            pltpu.VMEM((MAXB, BLK), F32),
        ],
        cost_estimate=cost(7),
        compiler_params=pltpu.CompilerParams(vmem_limit_bytes=16 * 2**20),
        name="partial_sums",
    )(info, counts, acts, grads, signs, u, vl, vj, low, high)


def finish_kernel(mine_ref, other_ref, q0_ref, q1_ref, q2_ref, q3_ref, proj_ref, score_ref, row_ref):
    ex = lax.axis_index("ex")
    proj = mine_ref[...] + other_ref[...]
    proj_ref[...] = proj
    for s in range(8):
        row_ref[s : s + 1, :] = proj[:, 512 * s : 512 * s + 512]
    acc = q0_ref[...] * row_ref[pl.ds(ex, 1), :]
    order = [0]
    for step, ref in zip(EX_STEPS, (q1_ref, q2_ref, q3_ref)):
        fresh = [d ^ step for d in order]
        for n, d in enumerate(fresh):
            acc = acc + ref[n] * row_ref[pl.ds(ex ^ d, 1), :]
        order = order + fresh
    acc = (acc[:, 0:128] + acc[:, 128:256]) + (acc[:, 256:384] + acc[:, 384:512])
    scores = lax.dot_general(
        jnp.ones((8, 128), F32), acc, NT, precision=lax.Precision.HIGHEST, preferred_element_type=F32
    )
    score_ref[...] = scores[0:1] * (1.0 / math.sqrt(PROJ))


def finish(mine, other, queries):
    vmem = pl.BlockSpec(memory_space=pltpu.VMEM)
    return pl.pallas_call(
        finish_kernel,
        out_shape=(
            jax.ShapeDtypeStruct((1, PROJ), F32),
            jax.ShapeDtypeStruct((1, 32), F32),
        ),
        in_specs=[vmem] * 6,
        out_specs=(vmem, vmem),
        scratch_shapes=[pltpu.VMEM((8, 512), F32)],
        compiler_params=pltpu.CompilerParams(vmem_limit_bytes=4 * 2**20),
        cost_estimate=cost(1),
        name="finish",
    )(mine, other, *queries)


def swap(value, axis, size, step):
    return lax.ppermute(value, axis, [(i, i ^ step) for i in range(size)])


def body(activations, output_grads, counts, sign_words, coord_row, coord_col, queries):
    grads = output_grads[0].T
    got = swap(activations, "feat", 32, ROW_STEPS[0])
    got_grads = swap(grads, "feat", 32, COL_STEPS[0])
    own = jnp.concatenate([activations[0], grads], axis=0)
    ints = jnp.concatenate(
        [(coord_row << 14) | coord_col, jnp.broadcast_to(counts, (8 * 128,))]
    ).reshape(40, 128)
    own, ints = lax.optimization_barrier((own, ints))
    place, info = rank_coords(ints, own)
    own, got, got_grads, _ = lax.optimization_barrier((own, got, got_grads, place))
    acts = jnp.concatenate([own[None, :TOK], got], axis=0)
    grads = jnp.concatenate([own[TOK:], got_grads], axis=0)
    got = swap(acts, "feat", 32, ROW_STEPS[1])
    got_grads = swap(grads, "feat", 32, COL_STEPS[1])
    signs = sign_table(sign_words.T, grads)
    sorted_fields, low, high = sort_coords(ints, place, grads, signs)
    acts, got, _ = lax.optimization_barrier((acts, got, sorted_fields))
    acts = jnp.concatenate([acts, got], axis=0)
    got = swap(acts, "feat", 32, ROW_STEPS[2])
    u, vl, vj = coord_signs(info, sorted_fields, acts)
    q, _ = lax.optimization_barrier((queries[None], acts))
    got_q = [swap(q, "ex", 8, EX_STEPS[0])]
    q = jnp.concatenate([q, got_q[-1]], axis=0)
    q, _ = lax.optimization_barrier((q, u))
    got_q.append(swap(q, "ex", 8, EX_STEPS[1]))
    q = jnp.concatenate([q, got_q[-1]], axis=0)
    acts = jnp.concatenate([acts, got], axis=0)
    grads = jnp.concatenate([grads, got_grads], axis=0)
    total = partial_sums(info, ints[32:], acts, grads, signs, u, vl, vj, low, high)
    for n, step in enumerate(SUM_STEPS[:-1]):
        total = total + swap(total, "feat", 32, step)
        if n == 0:
            q, total = lax.optimization_barrier((q, total))
            got_q.append(swap(q, "ex", 8, EX_STEPS[2]))
    other = swap(total, "feat", 32, SUM_STEPS[-1])
    return finish(total, other, [queries] + got_q)


def solution(mesh):
    return jax.shard_map(
        body,
        mesh=mesh,
        in_specs=(
            P("ex", None, "feat"),
            P("ex", None, "feat"),
            P("ex"),
            P(),
            P(),
            P(),
            P("feat", "ex"),
        ),
        out_specs=(P("ex", None), P("ex", "feat")),
        check_vma=False,
    )
```

```python
import math

import jax
import jax.numpy as jnp
from jax import lax
from jax.experimental import pallas as pl
from jax.experimental.pallas import tpu as pltpu
from jax.sharding import PartitionSpec as P

DIN = 4096
DPAD = 16384
PROJ = 4096
TOK = 128
COLS = 448
RUNS = COLS // 64
ROW_GROUPS = 8
COL_GROUPS = 8
GROUPS = ROW_GROUPS * COL_GROUPS
BLK = 128
MAXB = 96
UNROLL = 32
PIECES = 4
RUNS_HERE = PIECES * RUNS

ROW_STEPS = (16, 8, 6)
COL_STEPS = (2, 1)
PIECE = (0, 2, 1, 3)
SUM_STEPS = (1, 2, 6, 8, 16)
EX_STEPS = (4, 1, 3)

F32 = jnp.float32
BF16 = jnp.bfloat16
I32 = jnp.int32
NT = (((1,), (1,)), ((), ()))


def iota(shape, dim):
    return lax.broadcasted_iota(I32, shape, dim)


def parity(bits):
    bits = bits ^ (bits >> 4)
    bits = bits ^ (bits >> 2)
    bits = bits ^ (bits >> 1)
    return bits & 1


def parity3(bits):
    return (bits ^ (bits >> 1) ^ (bits >> 2)) & 1


def sign_of(bit):
    return (1 - 2 * bit).astype(F32)


def one_hot(cond):
    return jnp.where(cond, 1.0, 0.0)


def cost(microseconds):
    return pl.CostEstimate(
        flops=int(microseconds * 10**9), bytes_accessed=10**6, transcendentals=0
    )


def rank_kernel(ints_ref, after_ref, place_ref, info_ref, hot_ref, count_ref):
    coord = ints_ref[0:32, :]
    block_row = coord >> 21
    key = (
        ((coord >> 3) & 7)
        | (((block_row >> 4) & 1) << 3)
        | (((block_row >> 3) & 1) << 4)
        | ((((block_row >> 1) ^ (block_row >> 2)) & 1) << 5)
    )
    for i in range(32):
        hot_ref[GROUPS * i : GROUPS * i + GROUPS, :] = one_hot(
            iota((GROUPS, 128), 0) == key[i : i + 1]
        ).astype(BF16)
    lane = iota((128, 256), 1)
    upto = one_hot((iota((128, 256), 0) <= lane) | (lane >= 128)).astype(BF16)
    count_ref[...] = jnp.dot(hot_ref[...], upto, preferred_element_type=F32)
    total = jnp.zeros((GROUPS, 128), F32)
    for i in range(32):
        here = slice(GROUPS * i, GROUPS * i + GROUPS)
        count_ref[here, 0:128] = count_ref[here, 0:128] + total
        total = total + count_ref[here, 128:256]
    blocks = ((total.astype(I32) + (BLK - 1)) >> 7).astype(F32)
    earlier = one_hot(iota((GROUPS, GROUPS), 1) < iota((GROUPS, GROUPS), 0)).astype(BF16)
    base = jnp.dot(earlier, blocks.astype(BF16), preferred_element_type=F32)
    upto_here = base + blocks
    ended = one_hot(upto_here <= iota((GROUPS, 128), 1).astype(F32))
    owner = jnp.minimum(jnp.sum(ended, axis=0, keepdims=True), GROUPS - 1.0).astype(I32)
    used = upto_here[GROUPS - 1 : GROUPS].astype(I32)
    info_ref[...] = jnp.concatenate([owner, used, jnp.zeros((6, 128), I32)], axis=0)
    base = base * float(BLK) - 1.0
    for i in range(32):
        here = slice(GROUPS * i, GROUPS * i + GROUPS)
        spot = hot_ref[here, :].astype(F32) * (count_ref[here, 0:128] + base)
        place_ref[i : i + 1, :] = jnp.sum(spot, axis=0, keepdims=True).astype(I32)

def rank_coords(ints, after):
    return pl.pallas_call(
        rank_kernel,
        out_shape=(
            jax.ShapeDtypeStruct((32, 128), I32),
            jax.ShapeDtypeStruct((8, 128), I32),
        ),
        in_specs=[pl.BlockSpec(memory_space=pltpu.VMEM), pl.BlockSpec(memory_space=pl.ANY)],
        scratch_shapes=[
            pltpu.VMEM((GROUPS * 32, 128), BF16),
            pltpu.VMEM((GROUPS * 32, 256), F32),
        ],
        compiler_params=pltpu.CompilerParams(vmem_limit_bytes=8 * 2**20),
        cost_estimate=cost(1),
        name="rank_coords",
    )(ints, after)


def sort_kernel(
    coord_ref, place_ref, after_ref, after_too_ref, sorted_ref, low_ref, high_ref, value_ref
):
    for i in range(32):
        at = slice(128 * i, 128 * i + 128)
        spot, coord = place_ref[i : i + 1, :], coord_ref[i : i + 1, :]
        low_ref[:, at] = one_hot(iota((BLK, 128), 0) == (spot & (BLK - 1))).astype(BF16)
        high = one_hot(iota((MAXB, 128), 0) == (spot >> 7))
        high_ref[:, at] = high.astype(BF16)
        fields = ((coord >> 14) & 127, (coord >> 6) & 255, ((coord >> 21) << 3) | (coord & 7))
        for n, field in enumerate(fields):
            value_ref[MAXB * n : MAXB * n + MAXB, at] = (high * field.astype(F32)).astype(BF16)
    sorted_ref[...] = lax.dot_general(
        value_ref[...], low_ref[...], NT, preferred_element_type=F32
    ).astype(I32)


def sort_coords(coord, place, after, after_too):
    vmem = pl.BlockSpec(memory_space=pltpu.VMEM)
    return pl.pallas_call(
        sort_kernel,
        out_shape=(
            jax.ShapeDtypeStruct((3 * MAXB, BLK), I32),
            jax.ShapeDtypeStruct((BLK, PROJ), BF16),
            jax.ShapeDtypeStruct((MAXB, PROJ), BF16),
        ),
        in_specs=[vmem] * 2 + [pl.BlockSpec(memory_space=pl.ANY)] * 2,
        scratch_shapes=[pltpu.VMEM((3 * MAXB, PROJ), BF16)],
        compiler_params=pltpu.CompilerParams(vmem_limit_bytes=8 * 2**20),
        cost_estimate=cost(2),
        name="sort_coords",
    )(coord, place, after, after_too)


def block_signs(sorted_ref, b, run, feat):
    row = sorted_ref[pl.ds(b, 1), :]
    col_high = sorted_ref[pl.ds(MAXB + b, 1), :]
    rest = sorted_ref[pl.ds(2 * MAXB + b, 1), :]
    eight = iota((8, BLK), 0)
    column = [sign_of(parity3(eight & row))]
    for bit in range(3, 7):
        turn = sign_of((row >> bit) & 1)
        column = column + [part * turn for part in column]
    flip = parity((rest >> 3) & feat)
    scale = 1.0 / math.sqrt(DIN * DPAD)
    return (
        jnp.concatenate(column, axis=0).astype(BF16),
        sign_of(parity3(eight & rest) ^ flip) * scale,
        sign_of(parity(run & col_high)),
    )


def table_kernel(words_ref, after_ref, sign_ref):
    feat = lax.axis_index("feat")
    first_word = ((PIECES * COLS * (feat >> 2)) * 34953) >> 20
    words = words_ref[pl.ds(first_word, 64), :]
    octets = jnp.concatenate(
        [((words >> (8 * p)) & 255).astype(F32) for p in range(4)], axis=0
    ).astype(BF16)
    for e in range(PIECES):
        col = COLS * (feat ^ PIECE[e]) + iota((COLS, 128), 0)
        word = (col * 34953) >> 20
        bit = col - 30 * word
        target = ((bit >> 3) << 6) + (word - first_word)
        lane = iota((COLS, 128), 1)
        pick = jnp.concatenate(
            [one_hot(lane == target), one_hot(lane + 128 == target)], axis=1
        ).astype(BF16)
        octet = jnp.dot(pick, octets, preferred_element_type=F32).astype(I32)
        sign_ref[COLS * e : COLS * e + COLS, :] = sign_of((octet >> (bit & 7)) & 1)


def sign_table(words, after):
    return pl.pallas_call(
        table_kernel,
        out_shape=jax.ShapeDtypeStruct((PIECES * COLS, 128), F32),
        in_specs=[pl.BlockSpec(memory_space=pltpu.VMEM), pl.BlockSpec(memory_space=pl.ANY)],
        compiler_params=pltpu.CompilerParams(vmem_limit_bytes=8 * 2**20),
        cost_estimate=cost(2),
        name="sign_table",
    )(words, after)


def butterflies(parts):
    parts = list(parts)
    for bit in (1, 2, 4):
        for i in range(len(parts)):
            if not i & bit:
                one, two = parts[i], parts[i | bit]
                parts[i], parts[i | bit] = one + two, one - two
    return parts


def split(value):
    high = value.astype(BF16)
    return high, (value - high.astype(F32)).astype(BF16)


def main_kernel(
    info_ref, counts_ref, a_ref, g_ref, sign_ref, sorted_ref, low_ref, high_ref,
    out_ref, mixed_ref, signed_ref, block_ref,
):
    for first in range(0, TOK, 32):
        rows = slice(first, first + 32)
        parts = [a_ref[i, rows, :].astype(F32) for i in range(ROW_GROUPS)]
        live = first + iota((32, 128), 0) < counts_ref[0:1, 0:1]
        parts = [jnp.where(live, part, 0.0) for part in butterflies(parts)]
        for i in range(ROW_GROUPS):
            high, low = split(parts[i])
            mixed_ref[rows, 128 * i : 128 * i + 128] = high
            mixed_ref[TOK + first : TOK + first + 32, 128 * i : 128 * i + 128] = low
    tile = 2 * COLS
    for first in range(0, PIECES * COLS, tile):
        grads = g_ref[first : first + tile, :]
        grads = jnp.concatenate([grads, grads], axis=1)
        for pair in range(ROW_GROUPS // 2):
            outer = jnp.dot(
                grads, mixed_ref[:, 256 * pair : 256 * pair + 256], preferred_element_type=F32
            )
            for half in range(2):
                group = COL_GROUPS * (2 * pair + half)
                for at in range(0, tile, 128):
                    signed = (
                        outer[at : at + 128, 128 * half : 128 * half + 128]
                        * sign_ref[first + at : first + at + 128, :]
                    )
                    runs = [
                        butterflies(
                            [signed[64 * r + 8 * h : 64 * r + 8 * h + 8] for h in range(COL_GROUPS)]
                        )
                        for r in range(2)
                    ]
                    to = (first + at) // 8
                    for h in range(COL_GROUPS):
                        high, low = split(jnp.concatenate([runs[0][h], runs[1][h]], axis=0))
                        signed_ref[group + h, to : to + 16, 0:128] = high
                        signed_ref[group + h, to : to + 16, 128:256] = low
    block_ref[...] = jnp.zeros_like(block_ref)
    feat = lax.axis_index("feat")
    run = iota((32, BLK), 0)
    piece = (run * 37) >> 8
    run = RUNS * (feat ^ ((piece & 1) << 1) ^ (piece >> 1)) + (run - RUNS * piece)

    def step(i, carry):
        for n in range(UNROLL):
            b = i * UNROLL + n
            column, low_signs, run_signs = block_signs(sorted_ref, b, run, feat)
            weights = jnp.concatenate([column, column], axis=0)
            rows = jnp.dot(signed_ref[info_ref[0, b]], weights, preferred_element_type=F32)
            total = run_signs[0:1] * rows[0:8]
            for j in range(1, RUNS_HERE):
                total = total + run_signs[j : j + 1] * rows[8 * j : 8 * j + 8]
            block_ref[pl.ds(b, 1), :] = jnp.sum(total * low_signs, axis=0, keepdims=True)
        return carry

    lax.fori_loop(0, (info_ref[1, 0] + (UNROLL - 1)) // UNROLL, step, 0)
    pair = jnp.concatenate(split(block_ref[...]), axis=1)
    for first in range(0, PROJ, 512):
        at = slice(first, first + 512)
        low = low_ref[:, at]
        spread = jnp.dot(pair, jnp.concatenate([low, low], axis=0), preferred_element_type=F32)
        out_ref[:, at] = jnp.sum(spread * high_ref[:, at].astype(F32), axis=0, keepdims=True)


def partial_sums(info, counts, acts, grads, signs, sorted_fields, low, high):
    vmem = pl.BlockSpec(memory_space=pltpu.VMEM)
    return pl.pallas_call(
        main_kernel,
        out_shape=jax.ShapeDtypeStruct((1, PROJ), F32),
        in_specs=[pl.BlockSpec(memory_space=pltpu.SMEM)] + [vmem] * 7,
        out_specs=vmem,
        scratch_shapes=[
            pltpu.VMEM((2 * TOK, ROW_GROUPS * 128), BF16),
            pltpu.VMEM((GROUPS, RUNS_HERE * 8, 256), BF16),
            pltpu.VMEM((MAXB, BLK), F32),
        ],
        cost_estimate=cost(7),
        compiler_params=pltpu.CompilerParams(vmem_limit_bytes=16 * 2**20),
        name="partial_sums",
    )(info, counts, acts, grads, signs, sorted_fields, low, high)


def finish_kernel(mine_ref, other_ref, q0_ref, q1_ref, q2_ref, q3_ref, proj_ref, score_ref, row_ref):
    ex = lax.axis_index("ex")
    proj = mine_ref[...] + other_ref[...]
    proj_ref[...] = proj
    for s in range(8):
        row_ref[s : s + 1, :] = proj[:, 512 * s : 512 * s + 512]
    acc = q0_ref[...] * row_ref[pl.ds(ex, 1), :]
    order = [0]
    for step, ref in zip(EX_STEPS, (q1_ref, q2_ref, q3_ref)):
        fresh = [d ^ step for d in order]
        for n, d in enumerate(fresh):
            acc = acc + ref[n] * row_ref[pl.ds(ex ^ d, 1), :]
        order = order + fresh
    acc = (acc[:, 0:128] + acc[:, 128:256]) + (acc[:, 256:384] + acc[:, 384:512])
    scores = lax.dot_general(
        jnp.ones((8, 128), F32), acc, NT, precision=lax.Precision.HIGHEST, preferred_element_type=F32
    )
    score_ref[...] = scores[0:1] * (1.0 / math.sqrt(PROJ))


def finish(mine, other, queries):
    vmem = pl.BlockSpec(memory_space=pltpu.VMEM)
    return pl.pallas_call(
        finish_kernel,
        out_shape=(
            jax.ShapeDtypeStruct((1, PROJ), F32),
            jax.ShapeDtypeStruct((1, 32), F32),
        ),
        in_specs=[vmem] * 6,
        out_specs=(vmem, vmem),
        scratch_shapes=[pltpu.VMEM((8, 512), F32)],
        compiler_params=pltpu.CompilerParams(vmem_limit_bytes=4 * 2**20),
        cost_estimate=cost(1),
        name="finish",
    )(mine, other, *queries)


def join_kernel(*refs):
    parts, out_ref = refs[:-2], refs[-1]
    rows = out_ref.shape[0] // len(parts)
    for n, ref in enumerate(parts):
        out_ref[rows * n : rows * n + rows] = ref[...]


def join(parts, after):
    vmem = pl.BlockSpec(memory_space=pltpu.VMEM)
    shape = (len(parts) * parts[0].shape[0],) + parts[0].shape[1:]
    return pl.pallas_call(
        join_kernel,
        out_shape=jax.ShapeDtypeStruct(shape, parts[0].dtype),
        in_specs=[vmem] * len(parts) + [pl.BlockSpec(memory_space=pl.ANY)],
        out_specs=vmem,
        compiler_params=pltpu.CompilerParams(vmem_limit_bytes=2**20),
        cost_estimate=cost(1),
        name="join",
    )(*parts, after)


def swap(value, axis, size, step):
    return lax.ppermute(value, axis, [(i, i ^ step) for i in range(size)])


def body(activations, output_grads, counts, sign_words, coord_row, coord_col, queries):
    grads = output_grads[0].T
    got = swap(activations, "feat", 32, ROW_STEPS[0])
    got_grads = swap(grads, "feat", 32, COL_STEPS[0])
    own = jnp.concatenate([activations[0], grads], axis=0)
    ints = jnp.concatenate(
        [(coord_row << 14) | coord_col, jnp.broadcast_to(counts, (8 * 128,))]
    ).reshape(40, 128)
    own, ints = lax.optimization_barrier((own, ints))
    place, info = rank_coords(ints, own)
    own, got, _ = lax.optimization_barrier((own, got, place))
    acts = jnp.concatenate([own[None, :TOK], got], axis=0)
    grads = jnp.concatenate([own[TOK:], got_grads], axis=0)
    got = swap(acts, "feat", 32, ROW_STEPS[1])
    got_grads = swap(grads, "feat", 32, COL_STEPS[1])
    signs = sign_table(sign_words.T, acts)
    sorted_fields, low, high = sort_coords(ints, place, acts, signs)
    acts, got, _ = lax.optimization_barrier((acts, got, sorted_fields))
    acts = jnp.concatenate([acts, got], axis=0)
    got = swap(acts, "feat", 32, ROW_STEPS[2])
    q = join([queries[None]], acts)
    got_q = [swap(q, "ex", 8, EX_STEPS[0])]
    acts = jnp.concatenate([acts, got], axis=0)
    grads = jnp.concatenate([grads, got_grads], axis=0)
    total = partial_sums(info, ints[32:], acts, grads, signs, sorted_fields, low, high)
    for n, step in enumerate(SUM_STEPS[:-1]):
        total = total + swap(total, "feat", 32, step)
        if n in (0, 2):
            q, total = lax.optimization_barrier((jnp.concatenate([q, got_q[-1]], axis=0), total))
            got_q.append(swap(q, "ex", 8, EX_STEPS[len(got_q)]))
    other = swap(total, "feat", 32, SUM_STEPS[-1])
    return finish(total, other, [queries] + got_q)


def solution(mesh):
    return jax.shard_map(
        body,
        mesh=mesh,
        in_specs=(
            P("ex", None, "feat"),
            P("ex", None, "feat"),
            P("ex"),
            P(),
            P(),
            P(),
            P("feat", "ex"),
        ),
        out_specs=(P("ex", None), P("ex", "feat")),
        check_vma=False,
    )
```

```python
import math

import jax
import jax.numpy as jnp
from jax import lax
from jax.experimental import pallas as pl
from jax.experimental.pallas import tpu as pltpu
from jax.sharding import PartitionSpec as P

DIN = 4096
DPAD = 16384
PROJ = 4096
TOK = 128
COLS = 448
RUNS = COLS // 64
ROW_GROUPS = 8
COL_GROUPS = 8
GROUPS = ROW_GROUPS * COL_GROUPS
BLK = 128
MAXB = 96
UNROLL = 32
PIECES = 4
RUNS_HERE = PIECES * RUNS

ROW_STEPS = (16, 8, 6)
COL_STEPS = (2, 1)
PIECE = (0, 2, 1, 3)
SUM_STEPS = (1, 2, 6, 8, 16)
EX_STEPS = (4, 1, 3)

F32 = jnp.float32
BF16 = jnp.bfloat16
I32 = jnp.int32
NT = (((1,), (1,)), ((), ()))


def iota(shape, dim):
    return lax.broadcasted_iota(I32, shape, dim)


def parity(bits):
    bits = bits ^ (bits >> 4)
    bits = bits ^ (bits >> 2)
    bits = bits ^ (bits >> 1)
    return bits & 1


def parity3(bits):
    return (bits ^ (bits >> 1) ^ (bits >> 2)) & 1


def sign_of(bit):
    return (1 - 2 * bit).astype(F32)


def one_hot(cond):
    return jnp.where(cond, 1.0, 0.0)


def cost(microseconds):
    return pl.CostEstimate(
        flops=int(microseconds * 10**9), bytes_accessed=10**6, transcendentals=0
    )


def rank_kernel(ints_ref, after_ref, place_ref, info_ref, hot_ref, count_ref):
    coord = ints_ref[0:32, :]
    block_row = coord >> 21
    key = (
        ((coord >> 3) & 7)
        | (((block_row >> 4) & 1) << 3)
        | (((block_row >> 3) & 1) << 4)
        | ((((block_row >> 1) ^ (block_row >> 2)) & 1) << 5)
    )
    for i in range(32):
        hot_ref[GROUPS * i : GROUPS * i + GROUPS, :] = one_hot(
            iota((GROUPS, 128), 0) == key[i : i + 1]
        ).astype(BF16)
    lane = iota((128, 256), 1)
    upto = one_hot((iota((128, 256), 0) <= lane) | (lane >= 128)).astype(BF16)
    count_ref[...] = jnp.dot(hot_ref[...], upto, preferred_element_type=F32)
    total = jnp.zeros((GROUPS, 128), F32)
    for i in range(32):
        here = slice(GROUPS * i, GROUPS * i + GROUPS)
        count_ref[here, 0:128] = count_ref[here, 0:128] + total
        total = total + count_ref[here, 128:256]
    blocks = ((total.astype(I32) + (BLK - 1)) >> 7).astype(F32)
    earlier = one_hot(iota((GROUPS, GROUPS), 1) < iota((GROUPS, GROUPS), 0)).astype(BF16)
    base = jnp.dot(earlier, blocks.astype(BF16), preferred_element_type=F32)
    upto_here = base + blocks
    ended = one_hot(upto_here <= iota((GROUPS, 128), 1).astype(F32))
    owner = jnp.minimum(jnp.sum(ended, axis=0, keepdims=True), GROUPS - 1.0).astype(I32)
    used = upto_here[GROUPS - 1 : GROUPS].astype(I32)
    info_ref[...] = jnp.concatenate([owner, used, jnp.zeros((6, 128), I32)], axis=0)
    base = base * float(BLK) - 1.0
    for i in range(32):
        here = slice(GROUPS * i, GROUPS * i + GROUPS)
        spot = hot_ref[here, :].astype(F32) * (count_ref[here, 0:128] + base)
        place_ref[i : i + 1, :] = jnp.sum(spot, axis=0, keepdims=True).astype(I32)

def rank_coords(ints, after):
    return pl.pallas_call(
        rank_kernel,
        out_shape=(
            jax.ShapeDtypeStruct((32, 128), I32),
            jax.ShapeDtypeStruct((8, 128), I32),
        ),
        in_specs=[pl.BlockSpec(memory_space=pltpu.VMEM), pl.BlockSpec(memory_space=pl.ANY)],
        scratch_shapes=[
            pltpu.VMEM((GROUPS * 32, 128), BF16),
            pltpu.VMEM((GROUPS * 32, 256), F32),
        ],
        compiler_params=pltpu.CompilerParams(vmem_limit_bytes=8 * 2**20),
        cost_estimate=cost(1),
        name="rank_coords",
    )(ints, after)


def sort_kernel(
    coord_ref, place_ref, after_ref, after_too_ref, sorted_ref, low_ref, high_ref, value_ref
):
    for i in range(32):
        at = slice(128 * i, 128 * i + 128)
        spot, coord = place_ref[i : i + 1, :], coord_ref[i : i + 1, :]
        low_ref[:, at] = one_hot(iota((BLK, 128), 0) == (spot & (BLK - 1))).astype(BF16)
        high = one_hot(iota((MAXB, 128), 0) == (spot >> 7))
        high_ref[:, at] = high.astype(BF16)
        fields = ((coord >> 14) & 127, (coord >> 6) & 255, ((coord >> 21) << 3) | (coord & 7))
        for n, field in enumerate(fields):
            value_ref[MAXB * n : MAXB * n + MAXB, at] = (high * field.astype(F32)).astype(BF16)
    sorted_ref[...] = lax.dot_general(
        value_ref[...], low_ref[...], NT, preferred_element_type=F32
    ).astype(I32)


def sort_coords(coord, place, after, after_too):
    vmem = pl.BlockSpec(memory_space=pltpu.VMEM)
    return pl.pallas_call(
        sort_kernel,
        out_shape=(
            jax.ShapeDtypeStruct((3 * MAXB, BLK), I32),
            jax.ShapeDtypeStruct((BLK, PROJ), BF16),
            jax.ShapeDtypeStruct((MAXB, PROJ), BF16),
        ),
        in_specs=[vmem] * 2 + [pl.BlockSpec(memory_space=pl.ANY)] * 2,
        scratch_shapes=[pltpu.VMEM((3 * MAXB, PROJ), BF16)],
        compiler_params=pltpu.CompilerParams(vmem_limit_bytes=8 * 2**20),
        cost_estimate=cost(2),
        name="sort_coords",
    )(coord, place, after, after_too)


def block_signs(sorted_ref, b, run, feat):
    row = sorted_ref[pl.ds(b, 1), :]
    col_high = sorted_ref[pl.ds(MAXB + b, 1), :]
    rest = sorted_ref[pl.ds(2 * MAXB + b, 1), :]
    eight = iota((8, BLK), 0)
    column = [sign_of(parity3(eight & row))]
    for bit in range(3, 7):
        turn = sign_of((row >> bit) & 1)
        column = column + [part * turn for part in column]
    flip = parity((rest >> 3) & feat)
    scale = 1.0 / math.sqrt(DIN * DPAD)
    return (
        jnp.concatenate(column, axis=0).astype(BF16),
        sign_of(parity3(eight & rest) ^ flip) * scale,
        sign_of(parity(run & col_high)),
    )


def table_kernel(words_ref, after_ref, sign_ref):
    feat = lax.axis_index("feat")
    for e in range(PIECES):
        first_col = COLS * (feat ^ PIECE[e])
        first_word = (first_col * 34953) >> 20
        words = words_ref[pl.ds(first_word, 32), :]
        octets = jnp.concatenate(
            [((words >> (8 * p)) & 255).astype(F32) for p in range(4)], axis=0
        ).astype(BF16)
        col = first_col + iota((COLS, 128), 0)
        word = (col * 34953) >> 20
        bit = col - 30 * word
        target = ((bit >> 3) << 5) + (word - first_word)
        pick = one_hot(iota((COLS, 128), 1) == target).astype(BF16)
        octet = jnp.dot(pick, octets, preferred_element_type=F32).astype(I32)
        sign_ref[COLS * e : COLS * e + COLS, :] = sign_of((octet >> (bit & 7)) & 1)


def sign_table(words, after):
    return pl.pallas_call(
        table_kernel,
        out_shape=jax.ShapeDtypeStruct((PIECES * COLS, 128), F32),
        in_specs=[pl.BlockSpec(memory_space=pltpu.VMEM), pl.BlockSpec(memory_space=pl.ANY)],
        compiler_params=pltpu.CompilerParams(vmem_limit_bytes=8 * 2**20),
        cost_estimate=cost(2),
        name="sign_table",
    )(words, after)


def butterflies(parts):
    parts = list(parts)
    for bit in (1, 2, 4):
        for i in range(len(parts)):
            if not i & bit:
                one, two = parts[i], parts[i | bit]
                parts[i], parts[i | bit] = one + two, one - two
    return parts


def split(value):
    high = value.astype(BF16)
    return high, (value - high.astype(F32)).astype(BF16)


def main_kernel(
    info_ref, counts_ref, a_ref, g_ref, sign_ref, sorted_ref, low_ref, high_ref,
    out_ref, mixed_ref, signed_ref, block_ref,
):
    for first in range(0, TOK, 32):
        rows = slice(first, first + 32)
        parts = [a_ref[i, rows, :].astype(F32) for i in range(ROW_GROUPS)]
        live = first + iota((32, 128), 0) < counts_ref[0:1, 0:1]
        parts = [jnp.where(live, part, 0.0) for part in butterflies(parts)]
        for i in range(ROW_GROUPS):
            high, low = split(parts[i])
            mixed_ref[rows, 128 * i : 128 * i + 128] = high
            mixed_ref[TOK + first : TOK + first + 32, 128 * i : 128 * i + 128] = low
    tile = 2 * COLS
    for first in range(0, PIECES * COLS, tile):
        grads = g_ref[first : first + tile, :]
        grads = jnp.concatenate([grads, grads], axis=1)
        for pair in range(ROW_GROUPS // 2):
            outer = jnp.dot(
                grads, mixed_ref[:, 256 * pair : 256 * pair + 256], preferred_element_type=F32
            )
            for half in range(2):
                group = COL_GROUPS * (2 * pair + half)
                for at in range(0, tile, 128):
                    signed = (
                        outer[at : at + 128, 128 * half : 128 * half + 128]
                        * sign_ref[first + at : first + at + 128, :]
                    )
                    runs = [
                        butterflies(
                            [signed[64 * r + 8 * h : 64 * r + 8 * h + 8] for h in range(COL_GROUPS)]
                        )
                        for r in range(2)
                    ]
                    to = (first + at) // 8
                    for h in range(COL_GROUPS):
                        high, low = split(jnp.concatenate([runs[0][h], runs[1][h]], axis=0))
                        signed_ref[group + h, to : to + 16, 0:128] = high
                        signed_ref[group + h, to : to + 16, 128:256] = low
    block_ref[...] = jnp.zeros_like(block_ref)
    feat = lax.axis_index("feat")
    run = iota((32, BLK), 0)
    piece = (run * 37) >> 8
    run = RUNS * (feat ^ ((piece & 1) << 1) ^ (piece >> 1)) + (run - RUNS * piece)

    def step(i, carry):
        for n in range(UNROLL):
            b = i * UNROLL + n
            column, low_signs, run_signs = block_signs(sorted_ref, b, run, feat)
            weights = jnp.concatenate([column, column], axis=0)
            rows = jnp.dot(signed_ref[info_ref[0, b]], weights, preferred_element_type=F32)
            total = run_signs[0:1] * rows[0:8]
            for j in range(1, RUNS_HERE):
                total = total + run_signs[j : j + 1] * rows[8 * j : 8 * j + 8]
            block_ref[pl.ds(b, 1), :] = jnp.sum(total * low_signs, axis=0, keepdims=True)
        return carry

    lax.fori_loop(0, (info_ref[1, 0] + (UNROLL - 1)) // UNROLL, step, 0)
    pair = jnp.concatenate(split(block_ref[...]), axis=1)
    for first in range(0, PROJ, 512):
        at = slice(first, first + 512)
        low = low_ref[:, at]
        spread = jnp.dot(pair, jnp.concatenate([low, low], axis=0), preferred_element_type=F32)
        out_ref[:, at] = jnp.sum(spread * high_ref[:, at].astype(F32), axis=0, keepdims=True)


def partial_sums(info, counts, acts, grads, signs, sorted_fields, low, high):
    vmem = pl.BlockSpec(memory_space=pltpu.VMEM)
    return pl.pallas_call(
        main_kernel,
        out_shape=jax.ShapeDtypeStruct((1, PROJ), F32),
        in_specs=[pl.BlockSpec(memory_space=pltpu.SMEM)] + [vmem] * 7,
        out_specs=vmem,
        scratch_shapes=[
            pltpu.VMEM((2 * TOK, ROW_GROUPS * 128), BF16),
            pltpu.VMEM((GROUPS, RUNS_HERE * 8, 256), BF16),
            pltpu.VMEM((MAXB, BLK), F32),
        ],
        cost_estimate=cost(7),
        compiler_params=pltpu.CompilerParams(vmem_limit_bytes=16 * 2**20),
        name="partial_sums",
    )(info, counts, acts, grads, signs, sorted_fields, low, high)


def finish_kernel(mine_ref, other_ref, q0_ref, q1_ref, q2_ref, q3_ref, proj_ref, score_ref, row_ref):
    ex = lax.axis_index("ex")
    proj = mine_ref[...] + other_ref[...]
    proj_ref[...] = proj
    for s in range(8):
        row_ref[s : s + 1, :] = proj[:, 512 * s : 512 * s + 512]
    acc = q0_ref[...] * row_ref[pl.ds(ex, 1), :]
    order = [0]
    for step, ref in zip(EX_STEPS, (q1_ref, q2_ref, q3_ref)):
        fresh = [d ^ step for d in order]
        for n, d in enumerate(fresh):
            acc = acc + ref[n] * row_ref[pl.ds(ex ^ d, 1), :]
        order = order + fresh
    acc = (acc[:, 0:128] + acc[:, 128:256]) + (acc[:, 256:384] + acc[:, 384:512])
    scores = lax.dot_general(
        jnp.ones((8, 128), F32), acc, NT, precision=lax.Precision.HIGHEST, preferred_element_type=F32
    )
    score_ref[...] = scores[0:1] * (1.0 / math.sqrt(PROJ))


def finish(mine, other, queries):
    vmem = pl.BlockSpec(memory_space=pltpu.VMEM)
    return pl.pallas_call(
        finish_kernel,
        out_shape=(
            jax.ShapeDtypeStruct((1, PROJ), F32),
            jax.ShapeDtypeStruct((1, 32), F32),
        ),
        in_specs=[vmem] * 6,
        out_specs=(vmem, vmem),
        scratch_shapes=[pltpu.VMEM((8, 512), F32)],
        compiler_params=pltpu.CompilerParams(vmem_limit_bytes=4 * 2**20),
        cost_estimate=cost(1),
        name="finish",
    )(mine, other, *queries)


def join_kernel(*refs):
    parts, out_ref = refs[:-2], refs[-1]
    rows = out_ref.shape[0] // len(parts)
    for n, ref in enumerate(parts):
        out_ref[rows * n : rows * n + rows] = ref[...]


def join(parts, after):
    vmem = pl.BlockSpec(memory_space=pltpu.VMEM)
    shape = (len(parts) * parts[0].shape[0],) + parts[0].shape[1:]
    return pl.pallas_call(
        join_kernel,
        out_shape=jax.ShapeDtypeStruct(shape, parts[0].dtype),
        in_specs=[vmem] * len(parts) + [pl.BlockSpec(memory_space=pl.ANY)],
        out_specs=vmem,
        compiler_params=pltpu.CompilerParams(vmem_limit_bytes=2**20),
        cost_estimate=cost(1),
        name="join",
    )(*parts, after)


def swap(value, axis, size, step):
    return lax.ppermute(value, axis, [(i, i ^ step) for i in range(size)])


def body(activations, output_grads, counts, sign_words, coord_row, coord_col, queries):
    grads = output_grads[0].T
    got = swap(activations, "feat", 32, ROW_STEPS[0])
    got_grads = swap(grads, "feat", 32, COL_STEPS[0])
    own = jnp.concatenate([activations[0], grads], axis=0)
    ints = jnp.concatenate(
        [(coord_row << 14) | coord_col, jnp.broadcast_to(counts, (8 * 128,))]
    ).reshape(40, 128)
    own, ints = lax.optimization_barrier((own, ints))
    place, info = rank_coords(ints, own)
    own, got, _ = lax.optimization_barrier((own, got, place))
    acts = jnp.concatenate([own[None, :TOK], got], axis=0)
    grads = jnp.concatenate([own[TOK:], got_grads], axis=0)
    got = swap(acts, "feat", 32, ROW_STEPS[1])
    got_grads = swap(grads, "feat", 32, COL_STEPS[1])
    signs = sign_table(sign_words.T, acts)
    sorted_fields, low, high = sort_coords(ints, place, acts, signs)
    acts, got, _ = lax.optimization_barrier((acts, got, sorted_fields))
    acts = jnp.concatenate([acts, got], axis=0)
    got = swap(acts, "feat", 32, ROW_STEPS[2])
    q = join([queries[None]], acts)
    got_q = [swap(q, "ex", 8, EX_STEPS[0])]
    acts = jnp.concatenate([acts, got], axis=0)
    grads = jnp.concatenate([grads, got_grads], axis=0)
    total = partial_sums(info, ints[32:], acts, grads, signs, sorted_fields, low, high)
    for n, step in enumerate(SUM_STEPS[:-1]):
        total = total + swap(total, "feat", 32, step)
        if n in (0, 2):
            q, total = lax.optimization_barrier((jnp.concatenate([q, got_q[-1]], axis=0), total))
            got_q.append(swap(q, "ex", 8, EX_STEPS[len(got_q)]))
    other = swap(total, "feat", 32, SUM_STEPS[-1])
    return finish(total, other, [queries] + got_q)


def solution(mesh):
    return jax.shard_map(
        body,
        mesh=mesh,
        in_specs=(
            P("ex", None, "feat"),
            P("ex", None, "feat"),
            P("ex"),
            P(),
            P(),
            P(),
            P("feat", "ex"),
        ),
        out_specs=(P("ex", None), P("ex", "feat")),
        check_vma=False,
    )
```
